1024 devices in a mesh: node: 64 (over z_lo, y, core), feat: 16 (over z_hi, x).
Axes of the slice: x: 4, y: 8, z: 16 (z_hi: 4, z_lo: 4; z = z_hi * 4 + z_lo), core: 2. Of those that a mesh axis runs over, the one named last changes fastest.
Arguments:
- features: bfloat16 [256, 262144], P('feat', 'node'), may hold values from -6 to 6
- self_weight: bfloat16 [256, 256], replicated, may hold values from -0.375 to 0.375
- neigh_weight: bfloat16 [256, 256], replicated, may hold values from -0.375 to 0.375
- tiles: bfloat16 [64, 112, 128, 128], P('node'), may hold values from -0.5 to 0.5
- tile_src: int32 [64, 112], P('node'), may hold values from 0 to 31
- tile_dst: int32 [64, 112], P('node'), may hold values from 0 to 159
- tile_count: int32 [64], P('node'), may hold values from 28 to 112, as said below
- out_grad: bfloat16 [256, 262144], P(None, ('node', 'feat')), may hold values from -6 to 6
Outputs:
- output: bfloat16 [256, 262144], P(None, ('node', 'feat'))
- grad_features: bfloat16 [256, 262144], P('feat', 'node')
The draws below stay inside these ranges and needn't reach their ends.
Inputs may be any that keep to these rules, and one draw needn't show every extreme that they name: `tile_count`: some node block has all 112 slots live.
All inputs are finite; a program needn't handle non-finite values.
Results may differ from the reference program's by a relative error of at most 0.018.
Values may be sent and summed in bfloat16 or wider, within the bound.
No kernel may reach another device: no remote copies, remote signals or barrier semaphores. Data moves between devices by JAX's collectives and lax.ppermute only.
A program may use at most 32 MiB of HBM per device.

```python
import jax
import jax.numpy as jnp
from jax import lax

H = 256
TILE = 128
SPAN = 2
TILE_BLK = 32
TILE_DEV = 112
NODE_BLOCKS = 64
NODES = 262144


def draw_tile_count(key, part):
    key = jax.random.fold_in(key, 7)
    first, second = jax.random.split(key)
    counts = jax.random.randint(first, (NODE_BLOCKS,), TILE_DEV // 4, TILE_DEV + 1, dtype=jnp.int32)
    fullest = jax.random.randint(second, (), 0, NODE_BLOCKS, dtype=jnp.int32)
    return jnp.where(jnp.arange(NODE_BLOCKS, dtype=jnp.int32) == fullest, TILE_DEV, counts).astype(jnp.int32)


def place_ends(values, stream_key, smallest, top_value):
    longest = values.shape.index(max(values.shape))
    spots = []
    for shift in (0, 1):
        where = [jax.random.randint(jax.random.fold_in(stream_key, axis), (), 0, length) for axis, length in enumerate(values.shape)]
        where[longest] = (where[longest] + shift) % values.shape[longest]
        spots.append(tuple(where))
    return values.at[spots[0]].set(smallest).at[spots[1]].set(top_value)


def steps_of(rng, shape, cuts, smallest, high):
    gain = 1.0
    for position, parts in cuts:
        draws = jax.random.uniform(jax.random.fold_in(jax.random.fold_in(rng, 6), position), (parts,), jnp.float32, smallest / len(cuts), high / len(cuts))
        gain = gain * jnp.repeat(jnp.exp(draws), shape[position] // parts).reshape((-1,) + (1,) * (len(shape) - 1 - position))
    return gain


def gaussian(rng, extent, spread, bound, cuts=(), held_as=jnp.bfloat16):
    loudness = steps_of(rng, extent, cuts, -0.22, 0.18) if cuts else 1.0
    values = jax.random.normal(rng, extent, jnp.float32) * spread * loudness
    return jnp.minimum(jnp.maximum(values, -bound), bound).astype(held_as)


def setup_inputs(seed: int = 0) -> dict:
    splits = jax.random.split(jax.random.key(seed), 9)
    return {
        "features": gaussian(splits[0], (H, NODES), 1.0, 6.0, ((0, 16), (1, 64))),
        "self_weight": gaussian(splits[1], (H, H), H ** -0.5, 0.375),
        "neigh_weight": gaussian(splits[2], (H, H), H ** -0.5, 0.375),
        "tiles": gaussian(splits[3], (NODE_BLOCKS, TILE_DEV, TILE, TILE), TILE ** -0.5, 0.5, ((0, 64),)),
        "tile_src": place_ends(jax.random.randint(splits[4], (NODE_BLOCKS, TILE_DEV), 0, TILE_BLK), jax.random.fold_in(splits[4], 1), 0, TILE_BLK - 1).astype(jnp.int32),
        "tile_dst": place_ends(jax.random.randint(splits[5], (NODE_BLOCKS, TILE_DEV), 0, (2 * SPAN + 1) * TILE_BLK), jax.random.fold_in(splits[5], 1), 0, ((2 * SPAN + 1) * TILE_BLK) - 1).astype(jnp.int32),
        "tile_count": draw_tile_count(jax.random.fold_in(splits[8], 71), 0),
        "out_grad": gaussian(splits[7], (H, NODES), 1.0, 6.0, ((1, 1024),)),
    }


def reference(features, self_weight, neigh_weight, tiles, tile_src, tile_dst, tile_count, out_grad):
    block_nodes = TILE * TILE_BLK
    slots = (2 * SPAN + 1) * TILE_BLK
    xblocks = features.astype(jnp.float32).reshape(H, NODE_BLOCKS, TILE_BLK, TILE).transpose(1, 0, 2, 3)
    positions = jnp.arange(TILE_DEV, dtype=jnp.int32)

    def forward_block(index, total):
        local = lax.dynamic_index_in_dim(xblocks, index, 0, keepdims=False)
        picked = local[:, tile_src[index], :]
        weights = tiles[index].astype(jnp.float32)
        contrib = jnp.einsum('fst,sut->fsu', picked, weights)
        live = (positions < tile_count[index]).astype(jnp.float32)
        contrib = contrib * live[None, :, None]
        buffer = jnp.zeros((H, slots, TILE), jnp.float32).at[:, tile_dst[index], :].add(contrib)
        pieces = buffer.reshape(H, 2 * SPAN + 1, block_nodes)
        for offset in range(-SPAN, SPAN + 1):
            target = ((index + offset) % NODE_BLOCKS).astype(jnp.int32)
            total = total.at[target].add(pieces[:, offset + SPAN, :])
        return total

    summed = lax.fori_loop(0, NODE_BLOCKS, forward_block, jnp.zeros((NODE_BLOCKS, H, block_nodes), jnp.float32))
    aggregate = summed.transpose(1, 0, 2).reshape(H, NODES).astype(jnp.bfloat16)
    pre = jnp.dot(self_weight, features, preferred_element_type=jnp.float32) + jnp.dot(neigh_weight, aggregate, preferred_element_type=jnp.float32)
    sig = jax.nn.sigmoid(pre)
    output = (pre * sig).astype(jnp.bfloat16)
    grad_pre = (out_grad.astype(jnp.float32) * sig * (1.0 + pre * (1.0 - sig))).astype(jnp.bfloat16)
    grad_self = jnp.dot(self_weight.T, grad_pre, preferred_element_type=jnp.float32).astype(jnp.bfloat16)
    grad_aggregate = jnp.dot(neigh_weight.T, grad_pre, preferred_element_type=jnp.float32).astype(jnp.bfloat16)
    gblocks = grad_aggregate.astype(jnp.float32).reshape(H, NODE_BLOCKS, block_nodes).transpose(1, 0, 2)

    def backward_block(index):
        near = [lax.dynamic_index_in_dim(gblocks, ((index + offset) % NODE_BLOCKS).astype(jnp.int32), 0, keepdims=False) for offset in range(-SPAN, SPAN + 1)]
        gathered = jnp.stack(near, axis=1).reshape(H, slots, TILE)
        live = (positions < tile_count[index]).astype(jnp.float32)
        chosen = gathered[:, tile_dst[index], :] * live[None, :, None]
        back = jnp.einsum('fsu,sut->fst', chosen, tiles[index].astype(jnp.float32))
        result = jnp.zeros((H, TILE_BLK, TILE), jnp.float32).at[:, tile_src[index], :].add(back)
        return result.reshape(H, block_nodes)

    grad_neigh = lax.map(backward_block, jnp.arange(NODE_BLOCKS, dtype=jnp.int32))
    grad_neigh = grad_neigh.transpose(1, 0, 2).reshape(H, NODES)
    grad_features = (grad_self.astype(jnp.float32) + grad_neigh).astype(jnp.bfloat16)
    return output, grad_features
```

```python
import jax
import jax.numpy as jnp
from jax import lax
from jax.experimental import pallas as pl
from jax.experimental.pallas import tpu as pltpu
from jax.sharding import PartitionSpec as P

TILE = 128
SPAN = 2
BATCH = 8

VMEM = pl.BlockSpec(memory_space=pltpu.VMEM)
SMEM = pl.BlockSpec(memory_space=pltpu.SMEM)
HBM = pl.BlockSpec(memory_space=pltpu.HBM)


def from_behind(array, axis, by):
    count = lax.axis_size(axis)
    return lax.ppermute(array, axis, [(i, (i + by) % count) for i in range(count)])


def in_hbm(array):
    return pltpu.with_memory_space_constraint(array, pltpu.HBM)


def swapped(array):
    return lax.ppermute(array, "node", [(i, i ^ 1) for i in range(lax.axis_size("node"))])


def start_tiles(tiles_ref, held, sems):
    def start(i, _):
        rows = pl.ds(i * BATCH, BATCH)
        pltpu.make_async_copy(tiles_ref.at[rows], held.at[rows], sems.at[i]).start()
        return 0

    lax.fori_loop(0, held.shape[0] // BATCH, start, 0)


def wait_tiles(tiles_ref, held, sems, i):
    rows = pl.ds(i * BATCH, BATCH)
    pltpu.make_async_copy(tiles_ref.at[rows], held.at[rows], sems.at[i]).wait()


def forward_kernel(count_ref, src_hbm, dst_hbm, x_hbm, tiles_ref, *refs):
    far_left, near, own, far_right = refs[:4]
    src_ref, dst_ref, x_ref, held, xs, acc, small_sems, sems = refs[4:]
    small = [
        pltpu.make_async_copy(there, here, small_sems.at[i])
        for i, (there, here) in enumerate(
            ((x_hbm, x_ref), (src_hbm, src_ref), (dst_hbm, dst_ref))
        )
    ]
    for copy in small:
        copy.start()
    start_tiles(tiles_ref, held, sems)
    tile_blk = xs.shape[0]
    slots = acc.shape[0] - 1
    acc[...] = jnp.zeros_like(acc)
    for copy in small:
        copy.wait()
    for c in range(tile_blk):
        xs[c] = x_ref[:, c * TILE : (c + 1) * TILE]
    count = count_ref[0]

    def step(i, _):
        wait_tiles(tiles_ref, held, sems, i)
        parts = []
        for b in range(BATCH):
            s = i * BATCH + b
            parts.append(
                lax.dot_general(
                    xs[src_ref[0, s]],
                    held[s],
                    (((1,), (1,)), ((), ())),
                    preferred_element_type=jnp.float32,
                )
            )
        for b in range(BATCH):
            s = i * BATCH + b
            d = jnp.where(s < count, dst_ref[0, s], slots)
            acc[d] += parts[b]
        return 0

    lax.fori_loop(0, held.shape[0] // BATCH, step, 0)
    outs = (far_left, near.at[0], own, near.at[1], far_right)
    for k, out in enumerate(outs):
        for r in range(tile_blk):
            out[r // 2, :, (r % 2) * TILE : (r % 2 + 1) * TILE] = acc[k * tile_blk + r].astype(
                out.dtype
            )


def is_odd():
    return lax.rem(lax.axis_index("node"), 2) == 1


def relay_kernel(far_left, near, own, far_right, left_out, right_out, own_out):
    odd = is_odd()

    @pl.when(odd)
    def _():
        left_out[...] = (far_left[...].astype(jnp.float32) + near[0].astype(jnp.float32)).astype(
            left_out.dtype
        )
        right_out[...] = far_right[...]
        own_out[...] = own[...] + near[1].astype(jnp.float32)

    @pl.when(jnp.logical_not(odd))
    def _():
        left_out[...] = far_left[...]
        right_out[...] = (far_right[...].astype(jnp.float32) + near[1].astype(jnp.float32)).astype(
            right_out.dtype
        )
        own_out[...] = own[...] + near[0].astype(jnp.float32)


def choose_kernel(back_two, on_two, out_ref):
    odd = is_odd()

    @pl.when(odd)
    def _():
        out_ref[...] = back_two[...]

    @pl.when(jnp.logical_not(odd))
    def _():
        out_ref[...] = on_two[...]


def backward_kernel(
    src_ref,
    dst_ref,
    count_ref,
    both_ref,
    back_two,
    on_two,
    partner,
    passed,
    tiles_ref,
    out_ref,
    gs,
    acc,
):
    tile_blk = acc.shape[0]
    slots = gs.shape[0] - 1
    feat_rows = acc.shape[1]
    odd = is_odd()

    def lay(k, ref):
        for r in range(tile_blk):
            gs[k * tile_blk + r] = ref[r // 2, :, (r % 2) * TILE : (r % 2 + 1) * TILE]

    lay(0, back_two)
    lay(SPAN, both_ref.at[:, feat_rows:, :])
    lay(2 * SPAN, on_two)

    @pl.when(odd)
    def _():
        lay(SPAN - 1, partner)
        lay(SPAN + 1, passed)

    @pl.when(jnp.logical_not(odd))
    def _():
        lay(SPAN - 1, passed)
        lay(SPAN + 1, partner)

    gs[slots] = jnp.zeros(gs.shape[1:], gs.dtype)
    for r in range(tile_blk):
        acc[r] = both_ref[r // 2, :feat_rows, (r % 2) * TILE : (r % 2 + 1) * TILE].astype(jnp.float32)
    count = count_ref[0]

    def step(i, _):
        parts = []
        for b in range(BATCH):
            s = i * BATCH + b
            d = jnp.where(s < count, dst_ref[0, s], slots)
            parts.append(jnp.dot(gs[d], tiles_ref[s], preferred_element_type=jnp.float32))
        for b in range(BATCH):
            acc[src_ref[0, i * BATCH + b]] += parts[b]
        return 0

    lax.fori_loop(0, tiles_ref.shape[0] // BATCH, step, 0)
    for r in range(tile_blk):
        out_ref[:, r * TILE : (r + 1) * TILE] = acc[r].astype(out_ref.dtype)


def join_kernel(x_ref, *refs):
    pieces, out_ref = refs[:-1], refs[-1]
    rows = x_ref.shape[0]
    width = out_ref.shape[2]
    for j in range(out_ref.shape[0]):
        out_ref[j, :rows, :] = x_ref[:, j * width : (j + 1) * width]
        total = pieces[0][j].astype(jnp.float32)
        for piece in pieces[1:]:
            total = total + piece[j].astype(jnp.float32)
        out_ref[j, rows:, :] = total.astype(out_ref.dtype)


def dense_kernel(both_ref, ws_ref, wn_ref, og_ref, out_ref, grads_ref):
    groups, twice, width = both_ref.shape
    rows = twice // 2
    x = both_ref[:, :rows, :].reshape(groups * rows, width)
    agg = both_ref[:, rows:, :].reshape(groups * rows, width)
    ws, wn = ws_ref[...], wn_ref[...]
    pre = jnp.dot(ws, x, preferred_element_type=jnp.float32) + jnp.dot(
        wn, agg, preferred_element_type=jnp.float32
    )
    s = jax.nn.sigmoid(pre)
    out_ref[...] = (pre * s).astype(out_ref.dtype)
    grad_pre = (og_ref[...].astype(jnp.float32) * s * (1.0 + pre * (1.0 - s))).astype(jnp.bfloat16)
    turned = (((0,), (0,)), ((), ()))
    grad_self = lax.dot_general(ws, grad_pre, turned, preferred_element_type=jnp.float32)
    grad_agg = lax.dot_general(wn, grad_pre, turned, preferred_element_type=jnp.float32)
    grads_ref[:, :rows, :] = grad_self.astype(jnp.bfloat16).reshape(groups, rows, width)
    grads_ref[:, rows:, :] = grad_agg.astype(jnp.bfloat16).reshape(groups, rows, width)


def body(features, self_weight, neigh_weight, tiles, tile_src, tile_dst, tile_count, out_grad):
    feat_rows, block_nodes = features.shape
    tile_blk = block_nodes // TILE
    slots = (2 * SPAN + 1) * tile_blk
    slot_count = tiles.shape[1]
    groups = lax.axis_size("feat")
    width = block_nodes // groups
    piece = (groups, feat_rows, width)
    both = (groups, 2 * feat_rows, width)
    local_tiles = tiles[0]
    params = pltpu.CompilerParams(vmem_limit_bytes=24 * 1024 * 1024)
    held = pltpu.VMEM((slot_count, TILE, TILE), jnp.bfloat16)
    sems = pltpu.SemaphoreType.DMA((slot_count // BATCH,))
    tile_flops = 2 * slot_count * feat_rows * TILE * TILE
    tile_bytes = slot_count * TILE * TILE * 2

    bf16_piece = jax.ShapeDtypeStruct(piece, jnp.bfloat16)
    f32_piece = jax.ShapeDtypeStruct(piece, jnp.float32)
    far_left, near, own, far_right = pl.pallas_call(
        forward_kernel,
        out_shape=[
            bf16_piece,
            jax.ShapeDtypeStruct((2,) + piece, jnp.bfloat16),
            f32_piece,
            bf16_piece,
        ],
        in_specs=[SMEM] + [HBM] * 4,
        out_specs=[VMEM] * 4,
        scratch_shapes=[
            pltpu.SMEM(tile_src.shape, jnp.int32),
            pltpu.SMEM(tile_dst.shape, jnp.int32),
            pltpu.VMEM(features.shape, jnp.bfloat16),
            held,
            pltpu.VMEM((tile_blk, feat_rows, TILE), jnp.bfloat16),
            pltpu.VMEM((slots + 1, feat_rows, TILE), jnp.float32),
            pltpu.SemaphoreType.DMA((3,)),
            sems,
        ],
        compiler_params=params,
        cost_estimate=pl.CostEstimate(flops=tile_flops, bytes_accessed=tile_bytes, transcendentals=0),
        name="tiles_forward",
    )(tile_count, *(in_hbm(a) for a in (tile_src, tile_dst, features, local_tiles)))

    left, right, own = pl.pallas_call(
        relay_kernel,
        out_shape=[bf16_piece, bf16_piece, f32_piece],
        in_specs=[VMEM] * 4,
        out_specs=[VMEM] * 3,
        compiler_params=params,
        name="relay",
    )(far_left, swapped(near), own, far_right)
    beside = pl.pallas_call(
        join_kernel,
        out_shape=jax.ShapeDtypeStruct(both, jnp.bfloat16),
        in_specs=[VMEM] * 4,
        out_specs=VMEM,
        compiler_params=params,
        name="join",
    )(features, own, from_behind(left, "node", -SPAN), from_behind(right, "node", SPAN))
    rows = lax.all_to_all(beside, "feat", split_axis=0, concat_axis=0, tiled=True)
    output, grads = pl.pallas_call(
        dense_kernel,
        out_shape=[
            jax.ShapeDtypeStruct(out_grad.shape, jnp.bfloat16),
            jax.ShapeDtypeStruct(both, jnp.bfloat16),
        ],
        in_specs=[VMEM] * 4,
        out_specs=[VMEM] * 2,
        compiler_params=params,
        name="dense",
    )(rows, self_weight, neigh_weight, out_grad)
    cols = lax.all_to_all(grads, "feat", split_axis=0, concat_axis=0, tiled=True)
    agg = cols[:, feat_rows:, :]
    back_two = from_behind(agg, "node", SPAN)
    on_two = from_behind(agg, "node", -SPAN)
    partner = swapped(agg)
    passed = swapped(
        pl.pallas_call(
            choose_kernel,
            out_shape=bf16_piece,
            in_specs=[VMEM] * 2,
            out_specs=VMEM,
            compiler_params=params,
            name="choose",
        )(back_two, on_two)
    )
    grad_features = pl.pallas_call(
        backward_kernel,
        out_shape=jax.ShapeDtypeStruct(features.shape, jnp.bfloat16),
        in_specs=[SMEM] * 3 + [VMEM] * 6,
        out_specs=VMEM,
        scratch_shapes=[
            pltpu.VMEM((slots + 1, feat_rows, TILE), jnp.bfloat16),
            pltpu.VMEM((tile_blk, feat_rows, TILE), jnp.float32),
        ],
        compiler_params=params,
        cost_estimate=pl.CostEstimate(flops=tile_flops, bytes_accessed=tile_bytes, transcendentals=0),
        name="tiles_backward",
    )(
        tile_src, tile_dst, tile_count, cols, back_two, on_two, partner, passed, local_tiles
    )
    return (output, grad_features)


def solution(mesh):
    return jax.shard_map(
        body,
        mesh=mesh,
        in_specs=(
            P("feat", "node"),
            P(),
            P(),
            P("node", None, None, None),
            P("node", None),
            P("node", None),
            P("node"),
            P(None, ("node", "feat")),
        ),
        out_specs=(P(None, ("node", "feat")), P("feat", "node")),
        check_vma=False,
    )
```

```python
import jax
import jax.numpy as jnp
from jax import lax
from jax.experimental import pallas as pl
from jax.experimental.pallas import tpu as pltpu
from jax.sharding import PartitionSpec as P

TILE = 128
SPAN = 2
BATCH = 28

VMEM = pl.BlockSpec(memory_space=pltpu.VMEM)
SMEM = pl.BlockSpec(memory_space=pltpu.SMEM)
HBM = pl.BlockSpec(memory_space=pltpu.HBM)


def from_behind(array, axis, by):
    count = lax.axis_size(axis)
    return lax.ppermute(array, axis, [(i, (i + by) % count) for i in range(count)])


def in_hbm(array):
    return pltpu.with_memory_space_constraint(array, pltpu.HBM)


def swapped(array):
    return lax.ppermute(array, "node", [(i, i ^ 1) for i in range(lax.axis_size("node"))])


def batches_of(count):
    return lax.div(count + (BATCH - 1), BATCH)


def start_tiles(tiles_ref, held, sems, batches):
    def start(i, _):
        rows = pl.ds(i * BATCH, BATCH)
        pltpu.make_async_copy(tiles_ref.at[rows], held.at[rows], sems.at[i]).start()
        return 0

    lax.fori_loop(0, batches, start, 0)


def wait_tiles(tiles_ref, held, sems, i):
    rows = pl.ds(i * BATCH, BATCH)
    pltpu.make_async_copy(tiles_ref.at[rows], held.at[rows], sems.at[i]).wait()


def forward_kernel(count_ref, src_hbm, dst_hbm, x_hbm, tiles_ref, *refs):
    far_left, near, own, far_right, held = refs[:5]
    src_ref, dst_ref, x_ref, xs, acc, small_sems, sems = refs[5:]
    small = [
        pltpu.make_async_copy(there, here, small_sems.at[i])
        for i, (there, here) in enumerate(
            ((x_hbm, x_ref), (src_hbm, src_ref), (dst_hbm, dst_ref))
        )
    ]
    for copy in small:
        copy.start()
    count = count_ref[0]
    batches = batches_of(count)
    start_tiles(tiles_ref, held, sems, batches)
    tile_blk = xs.shape[0]
    slots = acc.shape[0] - 1
    acc[...] = jnp.zeros_like(acc)
    for copy in small:
        copy.wait()
    for c in range(tile_blk):
        xs[c] = x_ref[:, c * TILE : (c + 1) * TILE]

    def step(i, _):
        wait_tiles(tiles_ref, held, sems, i)
        parts = []
        for b in range(BATCH):
            s = i * BATCH + b
            parts.append(
                lax.dot_general(
                    xs[src_ref[0, s]],
                    held[s],
                    (((1,), (1,)), ((), ())),
                    preferred_element_type=jnp.float32,
                )
            )
        for b in range(BATCH):
            s = i * BATCH + b
            d = jnp.where(s < count, dst_ref[0, s], slots)
            acc[d] += parts[b]
        return 0

    lax.fori_loop(0, batches, step, 0)
    outs = (far_left, near.at[0], own, near.at[1], far_right)
    for k, out in enumerate(outs):
        for r in range(tile_blk):
            out[r // 2, :, (r % 2) * TILE : (r % 2 + 1) * TILE] = acc[k * tile_blk + r].astype(
                out.dtype
            )


def is_odd():
    return lax.rem(lax.axis_index("node"), 2) == 1


def relay_kernel(far_left, near, own, far_right, left_out, right_out, own_out):
    odd = is_odd()

    @pl.when(odd)
    def _():
        left_out[...] = (far_left[...].astype(jnp.float32) + near[0].astype(jnp.float32)).astype(
            left_out.dtype
        )
        right_out[...] = far_right[...]
        own_out[...] = own[...] + near[1].astype(jnp.float32)

    @pl.when(jnp.logical_not(odd))
    def _():
        left_out[...] = far_left[...]
        right_out[...] = (far_right[...].astype(jnp.float32) + near[1].astype(jnp.float32)).astype(
            right_out.dtype
        )
        own_out[...] = own[...] + near[0].astype(jnp.float32)


def choose_kernel(back_two, on_two, out_ref):
    odd = is_odd()

    @pl.when(odd)
    def _():
        out_ref[...] = back_two[...]

    @pl.when(jnp.logical_not(odd))
    def _():
        out_ref[...] = on_two[...]


def backward_kernel(
    src_ref,
    dst_ref,
    count_ref,
    both_ref,
    back_two,
    on_two,
    partner,
    passed,
    tiles_ref,
    out_ref,
    gs,
    acc,
):
    tile_blk = acc.shape[0]
    slots = gs.shape[0] - 1
    feat_rows = acc.shape[1]
    odd = is_odd()

    def lay(k, ref):
        for r in range(tile_blk):
            gs[k * tile_blk + r] = ref[r // 2, :, (r % 2) * TILE : (r % 2 + 1) * TILE]

    lay(0, back_two)
    lay(SPAN, both_ref.at[:, feat_rows:, :])
    lay(2 * SPAN, on_two)

    @pl.when(odd)
    def _():
        lay(SPAN - 1, partner)
        lay(SPAN + 1, passed)

    @pl.when(jnp.logical_not(odd))
    def _():
        lay(SPAN - 1, passed)
        lay(SPAN + 1, partner)

    gs[slots] = jnp.zeros(gs.shape[1:], gs.dtype)
    for r in range(tile_blk):
        acc[r] = both_ref[r // 2, :feat_rows, (r % 2) * TILE : (r % 2 + 1) * TILE].astype(jnp.float32)
    count = count_ref[0]

    def step(i, _):
        parts = []
        for b in range(BATCH):
            s = i * BATCH + b
            d = jnp.where(s < count, dst_ref[0, s], slots)
            parts.append(jnp.dot(gs[d], tiles_ref[s], preferred_element_type=jnp.float32))
        for b in range(BATCH):
            acc[src_ref[0, i * BATCH + b]] += parts[b]
        return 0

    lax.fori_loop(0, batches_of(count), step, 0)
    for r in range(tile_blk):
        out_ref[:, r * TILE : (r + 1) * TILE] = acc[r].astype(out_ref.dtype)


def join_kernel(x_ref, *refs):
    pieces, out_ref = refs[:-1], refs[-1]
    rows = x_ref.shape[0]
    width = out_ref.shape[2]
    for j in range(out_ref.shape[0]):
        out_ref[j, :rows, :] = x_ref[:, j * width : (j + 1) * width]
        total = pieces[0][j].astype(jnp.float32)
        for piece in pieces[1:]:
            total = total + piece[j].astype(jnp.float32)
        out_ref[j, rows:, :] = total.astype(out_ref.dtype)


def dense_kernel(both_ref, ws_ref, wn_ref, og_ref, out_ref, grads_ref):
    groups, twice, width = both_ref.shape
    rows = twice // 2
    x = both_ref[:, :rows, :].reshape(groups * rows, width)
    agg = both_ref[:, rows:, :].reshape(groups * rows, width)
    ws, wn = ws_ref[...], wn_ref[...]
    pre = jnp.dot(ws, x, preferred_element_type=jnp.float32) + jnp.dot(
        wn, agg, preferred_element_type=jnp.float32
    )
    s = jax.nn.sigmoid(pre)
    out_ref[...] = (pre * s).astype(out_ref.dtype)
    grad_pre = (og_ref[...].astype(jnp.float32) * s * (1.0 + pre * (1.0 - s))).astype(jnp.bfloat16)
    turned = (((0,), (0,)), ((), ()))
    grad_self = lax.dot_general(ws, grad_pre, turned, preferred_element_type=jnp.float32)
    grad_agg = lax.dot_general(wn, grad_pre, turned, preferred_element_type=jnp.float32)
    grads_ref[:, :rows, :] = grad_self.astype(jnp.bfloat16).reshape(groups, rows, width)
    grads_ref[:, rows:, :] = grad_agg.astype(jnp.bfloat16).reshape(groups, rows, width)


def body(features, self_weight, neigh_weight, tiles, tile_src, tile_dst, tile_count, out_grad):
    feat_rows, block_nodes = features.shape
    tile_blk = block_nodes // TILE
    slots = (2 * SPAN + 1) * tile_blk
    slot_count = tiles.shape[1]
    groups = lax.axis_size("feat")
    width = block_nodes // groups
    piece = (groups, feat_rows, width)
    both = (groups, 2 * feat_rows, width)
    local_tiles = tiles[0]
    params = pltpu.CompilerParams(vmem_limit_bytes=24 * 1024 * 1024)
    tile_flops = 2 * slot_count * feat_rows * TILE * TILE
    tile_bytes = slot_count * TILE * TILE * 2

    bf16_piece = jax.ShapeDtypeStruct(piece, jnp.bfloat16)
    f32_piece = jax.ShapeDtypeStruct(piece, jnp.float32)
    far_left, near, own, far_right, held = pl.pallas_call(
        forward_kernel,
        out_shape=[
            bf16_piece,
            jax.ShapeDtypeStruct((2,) + piece, jnp.bfloat16),
            f32_piece,
            bf16_piece,
            jax.ShapeDtypeStruct(local_tiles.shape, jnp.bfloat16),
        ],
        in_specs=[SMEM] + [HBM] * 4,
        out_specs=[VMEM] * 5,
        scratch_shapes=[
            pltpu.SMEM(tile_src.shape, jnp.int32),
            pltpu.SMEM(tile_dst.shape, jnp.int32),
            pltpu.VMEM(features.shape, jnp.bfloat16),
            pltpu.VMEM((tile_blk, feat_rows, TILE), jnp.bfloat16),
            pltpu.VMEM((slots + 1, feat_rows, TILE), jnp.float32),
            pltpu.SemaphoreType.DMA((3,)),
            pltpu.SemaphoreType.DMA((slot_count // BATCH,)),
        ],
        compiler_params=params,
        cost_estimate=pl.CostEstimate(flops=tile_flops, bytes_accessed=tile_bytes, transcendentals=0),
        name="tiles_forward",
    )(tile_count, *(in_hbm(a) for a in (tile_src, tile_dst, features, local_tiles)))

    left, right, own = pl.pallas_call(
        relay_kernel,
        out_shape=[bf16_piece, bf16_piece, f32_piece],
        in_specs=[VMEM] * 4,
        out_specs=[VMEM] * 3,
        compiler_params=params,
        name="relay",
    )(far_left, swapped(near), own, far_right)
    beside = pl.pallas_call(
        join_kernel,
        out_shape=jax.ShapeDtypeStruct(both, jnp.bfloat16),
        in_specs=[VMEM] * 4,
        out_specs=VMEM,
        compiler_params=params,
        name="join",
    )(features, own, from_behind(left, "node", -SPAN), from_behind(right, "node", SPAN))
    rows = lax.all_to_all(beside, "feat", split_axis=0, concat_axis=0, tiled=True)
    output, grads = pl.pallas_call(
        dense_kernel,
        out_shape=[
            jax.ShapeDtypeStruct(out_grad.shape, jnp.bfloat16),
            jax.ShapeDtypeStruct(both, jnp.bfloat16),
        ],
        in_specs=[VMEM] * 4,
        out_specs=[VMEM] * 2,
        compiler_params=params,
        name="dense",
    )(rows, self_weight, neigh_weight, out_grad)
    cols = lax.all_to_all(grads, "feat", split_axis=0, concat_axis=0, tiled=True)
    agg = cols[:, feat_rows:, :]
    back_two = from_behind(agg, "node", SPAN)
    on_two = from_behind(agg, "node", -SPAN)
    partner = swapped(agg)
    passed = swapped(
        pl.pallas_call(
            choose_kernel,
            out_shape=bf16_piece,
            in_specs=[VMEM] * 2,
            out_specs=VMEM,
            compiler_params=params,
            name="choose",
        )(back_two, on_two)
    )
    grad_features = pl.pallas_call(
        backward_kernel,
        out_shape=jax.ShapeDtypeStruct(features.shape, jnp.bfloat16),
        in_specs=[SMEM] * 3 + [VMEM] * 6,
        out_specs=VMEM,
        scratch_shapes=[
            pltpu.VMEM((slots + 1, feat_rows, TILE), jnp.bfloat16),
            pltpu.VMEM((tile_blk, feat_rows, TILE), jnp.float32),
        ],
        compiler_params=params,
        cost_estimate=pl.CostEstimate(flops=tile_flops, bytes_accessed=tile_bytes, transcendentals=0),
        name="tiles_backward",
    )(
        tile_src, tile_dst, tile_count, cols, back_two, on_two, partner, passed, held
    )
    return (output, grad_features)


def solution(mesh):
    return jax.shard_map(
        body,
        mesh=mesh,
        in_specs=(
            P("feat", "node"),
            P(),
            P(),
            P("node", None, None, None),
            P("node", None),
            P("node", None),
            P("node"),
            P(None, ("node", "feat")),
        ),
        out_specs=(P(None, ("node", "feat")), P("feat", "node")),
        check_vma=False,
    )
```

```python
import functools

import jax
import jax.numpy as jnp
from jax import lax
from jax.experimental import pallas as pl
from jax.experimental.pallas import tpu as pltpu
from jax.sharding import PartitionSpec as P

TILE = 128
SPAN = 2
BATCH = 28

VMEM = pl.BlockSpec(memory_space=pltpu.VMEM)
SMEM = pl.BlockSpec(memory_space=pltpu.SMEM)
HBM = pl.BlockSpec(memory_space=pltpu.HBM)


def chips_swapped(array, first):
    count = lax.axis_size("node")
    pairs = []
    for chip in range(first, count // 2, 2):
        for core in range(2):
            one, two = chip * 2 + core, (chip * 2 + 2 + core) % count
            pairs += [(one, two), (two, one)]
    return lax.ppermute(array, "node", sorted(pairs))


def in_hbm(array):
    return pltpu.with_memory_space_constraint(array, pltpu.HBM)


def swapped(array):
    return lax.ppermute(array, "node", [(i, i ^ 1) for i in range(lax.axis_size("node"))])


def batches_of(count):
    return lax.div(count + (BATCH - 1), BATCH)


def start_tiles(tiles_ref, held, sems, batches):
    def start(i, _):
        rows = pl.ds(i * BATCH, BATCH)
        pltpu.make_async_copy(tiles_ref.at[rows], held.at[rows], sems.at[i]).start()
        return 0

    lax.fori_loop(0, batches, start, 0)


def wait_tiles(tiles_ref, held, sems, i):
    rows = pl.ds(i * BATCH, BATCH)
    pltpu.make_async_copy(tiles_ref.at[rows], held.at[rows], sems.at[i]).wait()


def forward_kernel(count_ref, src_hbm, dst_hbm, x_hbm, tiles_ref, *refs):
    far_left, near, own, far_right, held = refs[:5]
    src_ref, dst_ref, x_ref, xs, acc, small_sems, sems = refs[5:]
    small = [
        pltpu.make_async_copy(there, here, small_sems.at[i])
        for i, (there, here) in enumerate(
            ((x_hbm, x_ref), (src_hbm, src_ref), (dst_hbm, dst_ref))
        )
    ]
    for copy in small:
        copy.start()
    count = count_ref[0]
    batches = batches_of(count)
    start_tiles(tiles_ref, held, sems, batches)
    tile_blk = xs.shape[0]
    slots = acc.shape[0] - 1
    acc[...] = jnp.zeros_like(acc)
    for copy in small:
        copy.wait()
    for c in range(tile_blk):
        xs[c] = x_ref[:, c * TILE : (c + 1) * TILE]

    def step(i, _):
        wait_tiles(tiles_ref, held, sems, i)
        parts = []
        for b in range(BATCH):
            s = i * BATCH + b
            parts.append(
                lax.dot_general(
                    xs[src_ref[0, s]],
                    held[s],
                    (((1,), (1,)), ((), ())),
                    preferred_element_type=jnp.float32,
                )
            )
        for b in range(BATCH):
            s = i * BATCH + b
            d = jnp.where(s < count, dst_ref[0, s], slots)
            acc[d] += parts[b]
        return 0

    lax.fori_loop(0, batches, step, 0)
    outs = (far_left, near.at[0], own, near.at[1], far_right)
    for k, out in enumerate(outs):
        for r in range(tile_blk):
            out[r // 2, :, (r % 2) * TILE : (r % 2 + 1) * TILE] = acc[k * tile_blk + r].astype(
                out.dtype
            )


def place():
    block = lax.axis_index("node")
    return lax.rem(block, 2) == 1, lax.rem(lax.div(block, 2), 2) == 1


def for_each_place(step):
    core, chip = place()
    for second_core in (False, True):
        for second_chip in (False, True):
            here = jnp.logical_and(core == second_core, chip == second_chip)
            pl.when(here)(functools.partial(step, second_core, second_chip))


def relay_kernel(far_left, near, own, far_right, in_pair_out, between_out, own_out):
    def step(second_core, second_chip):
        left_out, right_out = (in_pair_out, between_out) if second_chip else (between_out, in_pair_out)
        if second_core:
            left_out[...] = (far_left[...].astype(jnp.float32) + near[0].astype(jnp.float32)).astype(
                left_out.dtype
            )
            right_out[...] = far_right[...]
            own_out[...] = own[...] + near[1].astype(jnp.float32)
        else:
            left_out[...] = far_left[...]
            right_out[...] = (far_right[...].astype(jnp.float32) + near[1].astype(jnp.float32)).astype(
                right_out.dtype
            )
            own_out[...] = own[...] + near[0].astype(jnp.float32)

    for_each_place(step)


def choose_kernel(in_pair, between, out_ref):
    core, chip = place()

    @pl.when(core == chip)
    def _():
        out_ref[...] = in_pair[...]

    @pl.when(core != chip)
    def _():
        out_ref[...] = between[...]


def backward_kernel(
    src_ref,
    dst_ref,
    count_ref,
    both_ref,
    in_pair,
    between,
    partner,
    passed,
    tiles_ref,
    out_ref,
    gs,
    acc,
):
    tile_blk = acc.shape[0]
    slots = gs.shape[0] - 1
    feat_rows = acc.shape[1]

    def lay(k, ref):
        for r in range(tile_blk):
            gs[k * tile_blk + r] = ref[r // 2, :, (r % 2) * TILE : (r % 2 + 1) * TILE]

    def lay_all(second_core, second_chip):
        lay(0, in_pair if second_chip else between)
        lay(SPAN - 1, partner if second_core else passed)
        lay(SPAN + 1, passed if second_core else partner)
        lay(2 * SPAN, between if second_chip else in_pair)

    lay(SPAN, both_ref.at[:, feat_rows:, :])
    for_each_place(lay_all)
    gs[slots] = jnp.zeros(gs.shape[1:], gs.dtype)
    for r in range(tile_blk):
        acc[r] = both_ref[r // 2, :feat_rows, (r % 2) * TILE : (r % 2 + 1) * TILE].astype(jnp.float32)
    count = count_ref[0]

    def step(i, _):
        parts = []
        for b in range(BATCH):
            s = i * BATCH + b
            d = jnp.where(s < count, dst_ref[0, s], slots)
            parts.append(jnp.dot(gs[d], tiles_ref[s], preferred_element_type=jnp.float32))
        for b in range(BATCH):
            acc[src_ref[0, i * BATCH + b]] += parts[b]
        return 0

    lax.fori_loop(0, batches_of(count), step, 0)
    for r in range(tile_blk):
        out_ref[:, r * TILE : (r + 1) * TILE] = acc[r].astype(out_ref.dtype)


def join_kernel(x_ref, *refs):
    pieces, out_ref = refs[:-1], refs[-1]
    rows = x_ref.shape[0]
    width = out_ref.shape[2]
    for j in range(out_ref.shape[0]):
        out_ref[j, :rows, :] = x_ref[:, j * width : (j + 1) * width]
        total = pieces[0][j].astype(jnp.float32)
        for piece in pieces[1:]:
            total = total + piece[j].astype(jnp.float32)
        out_ref[j, rows:, :] = total.astype(out_ref.dtype)


def dense_kernel(both_ref, ws_ref, wn_ref, og_ref, out_ref, grads_ref):
    groups, twice, width = both_ref.shape
    rows = twice // 2
    x = both_ref[:, :rows, :].reshape(groups * rows, width)
    agg = both_ref[:, rows:, :].reshape(groups * rows, width)
    ws, wn = ws_ref[...], wn_ref[...]
    pre = jnp.dot(ws, x, preferred_element_type=jnp.float32) + jnp.dot(
        wn, agg, preferred_element_type=jnp.float32
    )
    s = jax.nn.sigmoid(pre)
    out_ref[...] = (pre * s).astype(out_ref.dtype)
    grad_pre = (og_ref[...].astype(jnp.float32) * s * (1.0 + pre * (1.0 - s))).astype(jnp.bfloat16)
    turned = (((0,), (0,)), ((), ()))
    grad_self = lax.dot_general(ws, grad_pre, turned, preferred_element_type=jnp.float32)
    grad_agg = lax.dot_general(wn, grad_pre, turned, preferred_element_type=jnp.float32)
    grads_ref[:, :rows, :] = grad_self.astype(jnp.bfloat16).reshape(groups, rows, width)
    grads_ref[:, rows:, :] = grad_agg.astype(jnp.bfloat16).reshape(groups, rows, width)


def body(features, self_weight, neigh_weight, tiles, tile_src, tile_dst, tile_count, out_grad):
    feat_rows, block_nodes = features.shape
    tile_blk = block_nodes // TILE
    slots = (2 * SPAN + 1) * tile_blk
    slot_count = tiles.shape[1]
    groups = lax.axis_size("feat")
    width = block_nodes // groups
    piece = (groups, feat_rows, width)
    both = (groups, 2 * feat_rows, width)
    local_tiles = tiles[0]
    params = pltpu.CompilerParams(vmem_limit_bytes=24 * 1024 * 1024)
    tile_flops = 2 * slot_count * feat_rows * TILE * TILE
    tile_bytes = slot_count * TILE * TILE * 2

    bf16_piece = jax.ShapeDtypeStruct(piece, jnp.bfloat16)
    f32_piece = jax.ShapeDtypeStruct(piece, jnp.float32)
    far_left, near, own, far_right, held = pl.pallas_call(
        forward_kernel,
        out_shape=[
            bf16_piece,
            jax.ShapeDtypeStruct((2,) + piece, jnp.bfloat16),
            f32_piece,
            bf16_piece,
            jax.ShapeDtypeStruct(local_tiles.shape, jnp.bfloat16),
        ],
        in_specs=[SMEM] + [HBM] * 4,
        out_specs=[VMEM] * 5,
        scratch_shapes=[
            pltpu.SMEM(tile_src.shape, jnp.int32),
            pltpu.SMEM(tile_dst.shape, jnp.int32),
            pltpu.VMEM(features.shape, jnp.bfloat16),
            pltpu.VMEM((tile_blk, feat_rows, TILE), jnp.bfloat16),
            pltpu.VMEM((slots + 1, feat_rows, TILE), jnp.float32),
            pltpu.SemaphoreType.DMA((3,)),
            pltpu.SemaphoreType.DMA((slot_count // BATCH,)),
        ],
        compiler_params=params,
        cost_estimate=pl.CostEstimate(flops=tile_flops, bytes_accessed=tile_bytes, transcendentals=0),
        name="tiles_forward",
    )(tile_count, *(in_hbm(a) for a in (tile_src, tile_dst, features, local_tiles)))

    in_pair, between, own = pl.pallas_call(
        relay_kernel,
        out_shape=[bf16_piece, bf16_piece, f32_piece],
        in_specs=[VMEM] * 4,
        out_specs=[VMEM] * 3,
        compiler_params=params,
        name="relay",
    )(far_left, swapped(near), own, far_right)
    beside = pl.pallas_call(
        join_kernel,
        out_shape=jax.ShapeDtypeStruct(both, jnp.bfloat16),
        in_specs=[VMEM] * 4,
        out_specs=VMEM,
        compiler_params=params,
        name="join",
    )(features, own, chips_swapped(in_pair, 0), chips_swapped(between, 1))
    rows = lax.all_to_all(beside, "feat", split_axis=0, concat_axis=0, tiled=True)
    output, grads = pl.pallas_call(
        dense_kernel,
        out_shape=[
            jax.ShapeDtypeStruct(out_grad.shape, jnp.bfloat16),
            jax.ShapeDtypeStruct(both, jnp.bfloat16),
        ],
        in_specs=[VMEM] * 4,
        out_specs=[VMEM] * 2,
        compiler_params=params,
        name="dense",
    )(rows, self_weight, neigh_weight, out_grad)
    cols = lax.all_to_all(grads, "feat", split_axis=0, concat_axis=0, tiled=True)
    agg = cols[:, feat_rows:, :]
    in_pair = chips_swapped(agg, 0)
    between = chips_swapped(agg, 1)
    partner = swapped(agg)
    passed = swapped(
        pl.pallas_call(
            choose_kernel,
            out_shape=bf16_piece,
            in_specs=[VMEM] * 2,
            out_specs=VMEM,
            compiler_params=params,
            name="choose",
        )(in_pair, between)
    )
    grad_features = pl.pallas_call(
        backward_kernel,
        out_shape=jax.ShapeDtypeStruct(features.shape, jnp.bfloat16),
        in_specs=[SMEM] * 3 + [VMEM] * 6,
        out_specs=VMEM,
        scratch_shapes=[
            pltpu.VMEM((slots + 1, feat_rows, TILE), jnp.bfloat16),
            pltpu.VMEM((tile_blk, feat_rows, TILE), jnp.float32),
        ],
        compiler_params=params,
        cost_estimate=pl.CostEstimate(flops=tile_flops, bytes_accessed=tile_bytes, transcendentals=0),
        name="tiles_backward",
    )(
        tile_src, tile_dst, tile_count, cols, in_pair, between, partner, passed, held
    )
    return (output, grad_features)


def solution(mesh):
    return jax.shard_map(
        body,
        mesh=mesh,
        in_specs=(
            P("feat", "node"),
            P(),
            P(),
            P("node", None, None, None),
            P("node", None),
            P("node", None),
            P("node"),
            P(None, ("node", "feat")),
        ),
        out_specs=(P(None, ("node", "feat")), P("feat", "node")),
        check_vma=False,
    )
```

```python
import functools

import jax
import jax.numpy as jnp
from jax import lax
from jax.experimental import pallas as pl
from jax.experimental.pallas import tpu as pltpu
from jax.sharding import PartitionSpec as P

TILE = 128
SPAN = 2
BATCH = 28

VMEM = pl.BlockSpec(memory_space=pltpu.VMEM)
SMEM = pl.BlockSpec(memory_space=pltpu.SMEM)
HBM = pl.BlockSpec(memory_space=pltpu.HBM)


def chips_swapped(array, first):
    count = lax.axis_size("node")
    pairs = []
    for chip in range(first, count // 2, 2):
        for core in range(2):
            one, two = chip * 2 + core, (chip * 2 + 2 + core) % count
            pairs += [(one, two), (two, one)]
    return lax.ppermute(array, "node", sorted(pairs))


def in_hbm(array):
    return pltpu.with_memory_space_constraint(array, pltpu.HBM)


def swapped(array):
    return lax.ppermute(array, "node", [(i, i ^ 1) for i in range(lax.axis_size("node"))])


def batches_of(count):
    return lax.div(count + (BATCH - 1), BATCH)


def start_tiles(tiles_ref, held, sems, batches):
    def start(i, _):
        rows = pl.ds(i * BATCH, BATCH)
        pltpu.make_async_copy(tiles_ref.at[rows], held.at[rows], sems.at[i]).start()
        return 0

    lax.fori_loop(0, batches, start, 0)


def wait_tiles(tiles_ref, held, sems, i):
    rows = pl.ds(i * BATCH, BATCH)
    pltpu.make_async_copy(tiles_ref.at[rows], held.at[rows], sems.at[i]).wait()


def forward_kernel(count_ref, src_hbm, dst_hbm, x_hbm, tiles_ref, *refs):
    far_left, near, own, far_right, held = refs[:5]
    src_ref, dst_ref, x_ref, xs, acc, small_sems, sems = refs[5:]
    small = [
        pltpu.make_async_copy(there, here, small_sems.at[i])
        for i, (there, here) in enumerate(
            ((x_hbm, x_ref), (src_hbm, src_ref), (dst_hbm, dst_ref))
        )
    ]
    for copy in small:
        copy.start()
    count = count_ref[0]
    batches = batches_of(count)
    start_tiles(tiles_ref, held, sems, batches)
    tile_blk = xs.shape[0]
    slots = acc.shape[0] - 1
    acc[...] = jnp.zeros_like(acc)
    for copy in small:
        copy.wait()
    for c in range(tile_blk):
        xs[c] = x_ref[:, c * TILE : (c + 1) * TILE]

    def step(i, _):
        wait_tiles(tiles_ref, held, sems, i)
        parts = []
        for b in range(BATCH):
            s = i * BATCH + b
            parts.append(
                lax.dot_general(
                    xs[src_ref[0, s]],
                    held[s],
                    (((1,), (1,)), ((), ())),
                    preferred_element_type=jnp.float32,
                )
            )
        for b in range(BATCH):
            s = i * BATCH + b
            d = jnp.where(s < count, dst_ref[0, s], slots)
            acc[d] += parts[b]
        return 0

    lax.fori_loop(0, batches, step, 0)
    outs = (far_left, near.at[0], own, near.at[1], far_right)
    for k, out in enumerate(outs):
        for r in range(tile_blk):
            out[r // 2, :, (r % 2) * TILE : (r % 2 + 1) * TILE] = acc[k * tile_blk + r].astype(
                out.dtype
            )


def place():
    block = lax.axis_index("node")
    return lax.rem(block, 2) == 1, lax.rem(lax.div(block, 2), 2) == 1


def for_each_place(step):
    core, chip = place()
    for second_core in (False, True):
        for second_chip in (False, True):
            here = jnp.logical_and(core == second_core, chip == second_chip)
            pl.when(here)(functools.partial(step, second_core, second_chip))


def relay_kernel(far_left, near, own, far_right, in_pair_out, between_out, own_out):
    def step(second_core, second_chip):
        left_out, right_out = (in_pair_out, between_out) if second_chip else (between_out, in_pair_out)
        if second_core:
            left_out[...] = (far_left[...].astype(jnp.float32) + near[0].astype(jnp.float32)).astype(
                left_out.dtype
            )
            right_out[...] = far_right[...]
            own_out[...] = own[...] + near[1].astype(jnp.float32)
        else:
            left_out[...] = far_left[...]
            right_out[...] = (far_right[...].astype(jnp.float32) + near[1].astype(jnp.float32)).astype(
                right_out.dtype
            )
            own_out[...] = own[...] + near[0].astype(jnp.float32)

    for_each_place(step)


def choose_kernel(in_pair, between, out_ref):
    core, chip = place()

    @pl.when(core == chip)
    def _():
        out_ref[...] = in_pair[...]

    @pl.when(core != chip)
    def _():
        out_ref[...] = between[...]


def backward_kernel(
    src_ref,
    dst_ref,
    count_ref,
    both_ref,
    in_pair,
    between,
    partner,
    passed,
    tiles_ref,
    out_ref,
    gs,
    acc,
):
    tile_blk = acc.shape[0]
    slots = gs.shape[0] - 1
    feat_rows = acc.shape[1]

    def lay(k, ref):
        for r in range(tile_blk):
            gs[k * tile_blk + r] = ref[r // 2, :, (r % 2) * TILE : (r % 2 + 1) * TILE]

    def lay_all(second_core, second_chip):
        lay(0, in_pair if second_chip else between)
        lay(SPAN - 1, partner if second_core else passed)
        lay(SPAN + 1, passed if second_core else partner)
        lay(2 * SPAN, between if second_chip else in_pair)

    lay(SPAN, both_ref.at[:, feat_rows:, :])
    for_each_place(lay_all)
    gs[slots] = jnp.zeros(gs.shape[1:], gs.dtype)
    for r in range(tile_blk):
        acc[r] = both_ref[r // 2, :feat_rows, (r % 2) * TILE : (r % 2 + 1) * TILE].astype(jnp.float32)
    count = count_ref[0]

    def step(i, _):
        parts = []
        for b in range(BATCH):
            s = i * BATCH + b
            d = jnp.where(s < count, dst_ref[0, s], slots)
            parts.append(jnp.dot(gs[d], tiles_ref[s], preferred_element_type=jnp.float32))
        for b in range(BATCH):
            acc[src_ref[0, i * BATCH + b]] += parts[b]
        return 0

    lax.fori_loop(0, batches_of(count), step, 0)
    for r in range(tile_blk):
        out_ref[:, r * TILE : (r + 1) * TILE] = acc[r].astype(out_ref.dtype)


def join_kernel(x_ref, *refs):
    pieces, out_ref = refs[:-1], refs[-1]
    rows = x_ref.shape[0]
    width = out_ref.shape[2]
    for j in range(out_ref.shape[0]):
        out_ref[j, :rows, :] = x_ref[:, j * width : (j + 1) * width]
        total = pieces[0][j].astype(jnp.float32)
        for piece in pieces[1:]:
            total = total + piece[j].astype(jnp.float32)
        out_ref[j, rows:, :] = total.astype(out_ref.dtype)


def dense_kernel(both_ref, ws_ref, wn_ref, og_ref, out_ref, grads_ref):
    groups, twice, width = both_ref.shape
    rows = twice // 2
    x = both_ref[:, :rows, :].reshape(groups * rows, width)
    agg = both_ref[:, rows:, :].reshape(groups * rows, width)
    ws, wn = ws_ref[...], wn_ref[...]
    pre = jnp.dot(ws, x, preferred_element_type=jnp.float32) + jnp.dot(
        wn, agg, preferred_element_type=jnp.float32
    )
    s = jax.nn.sigmoid(pre)
    out_ref[...] = (pre * s).astype(out_ref.dtype)
    grad_pre = (og_ref[...].astype(jnp.float32) * s * (1.0 + pre * (1.0 - s))).astype(jnp.bfloat16)
    turned = (((0,), (0,)), ((), ()))
    grad_self = lax.dot_general(ws, grad_pre, turned, preferred_element_type=jnp.float32)
    grad_agg = lax.dot_general(wn, grad_pre, turned, preferred_element_type=jnp.float32)
    grads_ref[:, :rows, :] = grad_self.astype(jnp.bfloat16).reshape(groups, rows, width)
    grads_ref[:, rows:, :] = grad_agg.astype(jnp.bfloat16).reshape(groups, rows, width)


def body(features, self_weight, neigh_weight, tiles, tile_src, tile_dst, tile_count, out_grad):
    feat_rows, block_nodes = features.shape
    tile_blk = block_nodes // TILE
    slots = (2 * SPAN + 1) * tile_blk
    slot_count = tiles.shape[1]
    groups = lax.axis_size("feat")
    width = block_nodes // groups
    piece = (groups, feat_rows, width)
    both = (groups, 2 * feat_rows, width)
    local_tiles = tiles[0]
    params = pltpu.CompilerParams(vmem_limit_bytes=24 * 1024 * 1024)
    tile_flops = 2 * slot_count * feat_rows * TILE * TILE
    tile_bytes = slot_count * TILE * TILE * 2

    bf16_piece = jax.ShapeDtypeStruct(piece, jnp.bfloat16)
    f32_piece = jax.ShapeDtypeStruct(piece, jnp.float32)
    far_left, near, own, far_right, held = pl.pallas_call(
        forward_kernel,
        out_shape=[
            bf16_piece,
            jax.ShapeDtypeStruct((2,) + piece, jnp.bfloat16),
            f32_piece,
            bf16_piece,
            jax.ShapeDtypeStruct(local_tiles.shape, jnp.bfloat16),
        ],
        in_specs=[SMEM] + [HBM] * 4,
        out_specs=[VMEM] * 5,
        scratch_shapes=[
            pltpu.SMEM(tile_src.shape, jnp.int32),
            pltpu.SMEM(tile_dst.shape, jnp.int32),
            pltpu.VMEM(features.shape, jnp.bfloat16),
            pltpu.VMEM((tile_blk, feat_rows, TILE), jnp.bfloat16),
            pltpu.VMEM((slots + 1, feat_rows, TILE), jnp.float32),
            pltpu.SemaphoreType.DMA((3,)),
            pltpu.SemaphoreType.DMA((slot_count // BATCH,)),
        ],
        compiler_params=params,
        cost_estimate=pl.CostEstimate(flops=tile_flops, bytes_accessed=tile_bytes, transcendentals=0),
        name="tiles_forward",
    )(tile_count, *(in_hbm(a) for a in (tile_src, tile_dst, features, local_tiles)))

    in_pair, between, own = pl.pallas_call(
        relay_kernel,
        out_shape=[bf16_piece, bf16_piece, f32_piece],
        in_specs=[VMEM] * 4,
        out_specs=[VMEM] * 3,
        compiler_params=params,
        name="relay",
    )(far_left, swapped(near), own, far_right)
    beside = pl.pallas_call(
        join_kernel,
        out_shape=jax.ShapeDtypeStruct(both, jnp.bfloat16),
        in_specs=[VMEM] * 4,
        out_specs=VMEM,
        compiler_params=params,
        name="join",
    )(features, own, chips_swapped(between, 1), chips_swapped(in_pair, 0))
    rows = lax.all_to_all(beside, "feat", split_axis=0, concat_axis=0, tiled=True)
    output, grads = pl.pallas_call(
        dense_kernel,
        out_shape=[
            jax.ShapeDtypeStruct(out_grad.shape, jnp.bfloat16),
            jax.ShapeDtypeStruct(both, jnp.bfloat16),
        ],
        in_specs=[VMEM] * 4,
        out_specs=[VMEM] * 2,
        compiler_params=params,
        name="dense",
    )(rows, self_weight, neigh_weight, out_grad)
    cols = lax.all_to_all(grads, "feat", split_axis=0, concat_axis=0, tiled=True)
    agg = cols[:, feat_rows:, :]
    in_pair = chips_swapped(agg, 0)
    between = chips_swapped(agg, 1)
    partner = swapped(agg)
    passed = swapped(
        pl.pallas_call(
            choose_kernel,
            out_shape=bf16_piece,
            in_specs=[VMEM] * 2,
            out_specs=VMEM,
            compiler_params=params,
            name="choose",
        )(in_pair, between)
    )
    grad_features = pl.pallas_call(
        backward_kernel,
        out_shape=jax.ShapeDtypeStruct(features.shape, jnp.bfloat16),
        in_specs=[SMEM] * 3 + [VMEM] * 6,
        out_specs=VMEM,
        scratch_shapes=[
            pltpu.VMEM((slots + 1, feat_rows, TILE), jnp.bfloat16),
            pltpu.VMEM((tile_blk, feat_rows, TILE), jnp.float32),
        ],
        compiler_params=params,
        cost_estimate=pl.CostEstimate(flops=tile_flops, bytes_accessed=tile_bytes, transcendentals=0),
        name="tiles_backward",
    )(
        tile_src, tile_dst, tile_count, cols, in_pair, between, partner, passed, held
    )
    return (output, grad_features)


def solution(mesh):
    return jax.shard_map(
        body,
        mesh=mesh,
        in_specs=(
            P("feat", "node"),
            P(),
            P(),
            P("node", None, None, None),
            P("node", None),
            P("node", None),
            P("node"),
            P(None, ("node", "feat")),
        ),
        out_specs=(P(None, ("node", "feat")), P("feat", "node")),
        check_vma=False,
    )
```

```python
import functools

import jax
import jax.numpy as jnp
from jax import lax
from jax.experimental import pallas as pl
from jax.experimental.pallas import tpu as pltpu
from jax.sharding import PartitionSpec as P

TILE = 128
SPAN = 2
BATCH = 28

VMEM = pl.BlockSpec(memory_space=pltpu.VMEM)
SMEM = pl.BlockSpec(memory_space=pltpu.SMEM)
HBM = pl.BlockSpec(memory_space=pltpu.HBM)


def chips_swapped(array, first):
    count = lax.axis_size("node")
    pairs = []
    for chip in range(first, count // 2, 2):
        for core in range(2):
            one, two = chip * 2 + core, (chip * 2 + 2 + core) % count
            pairs += [(one, two), (two, one)]
    return lax.ppermute(array, "node", sorted(pairs))


def in_hbm(array):
    return pltpu.with_memory_space_constraint(array, pltpu.HBM)


def swapped(array):
    return lax.ppermute(array, "node", [(i, i ^ 1) for i in range(lax.axis_size("node"))])


def batches_of(count):
    return lax.div(count + (BATCH - 1), BATCH)


def start_tiles(tiles_ref, held, sems, batches):
    def start(i, _):
        rows = pl.ds(i * BATCH, BATCH)
        pltpu.make_async_copy(tiles_ref.at[rows], held.at[rows], sems.at[i]).start()
        return 0

    lax.fori_loop(0, batches, start, 0)


def wait_tiles(tiles_ref, held, sems, i):
    rows = pl.ds(i * BATCH, BATCH)
    pltpu.make_async_copy(tiles_ref.at[rows], held.at[rows], sems.at[i]).wait()


def forward_kernel(count_ref, src_hbm, dst_hbm, x_hbm, tiles_ref, *refs):
    far_left, near, own, far_right, held = refs[:5]
    src_ref, dst_ref, x_ref, xs, acc, small_sems, sems = refs[5:]
    small = [
        pltpu.make_async_copy(there, here, small_sems.at[i])
        for i, (there, here) in enumerate(
            ((x_hbm, x_ref), (src_hbm, src_ref), (dst_hbm, dst_ref))
        )
    ]
    for copy in small:
        copy.start()
    count = count_ref[0]
    batches = batches_of(count)
    start_tiles(tiles_ref, held, sems, batches)
    tile_blk = xs.shape[0]
    slots = acc.shape[0] - 1
    acc[...] = jnp.zeros_like(acc)
    for copy in small:
        copy.wait()
    for c in range(tile_blk):
        xs[c] = x_ref[:, c * TILE : (c + 1) * TILE]

    def step(i, _):
        wait_tiles(tiles_ref, held, sems, i)
        parts = []
        for b in range(BATCH):
            s = i * BATCH + b
            parts.append(
                lax.dot_general(
                    xs[src_ref[0, s]],
                    held[s],
                    (((1,), (1,)), ((), ())),
                    preferred_element_type=jnp.float32,
                )
            )
        for b in range(BATCH):
            s = i * BATCH + b
            d = jnp.where(s < count, dst_ref[0, s], slots)
            acc[d] += parts[b]
        return 0

    lax.fori_loop(0, batches, step, 0)
    outs = (far_left, near.at[0], own, near.at[1], far_right)
    for k, out in enumerate(outs):
        for r in range(tile_blk):
            out[r // 2, :, (r % 2) * TILE : (r % 2 + 1) * TILE] = acc[k * tile_blk + r].astype(
                out.dtype
            )


def place():
    block = lax.axis_index("node")
    return lax.rem(block, 2) == 1, lax.rem(lax.div(block, 2), 2) == 1


def for_each_place(step):
    core, chip = place()
    for second_core in (False, True):
        for second_chip in (False, True):
            here = jnp.logical_and(core == second_core, chip == second_chip)
            pl.when(here)(functools.partial(step, second_core, second_chip))


def relay_kernel(far_left, near, own, far_right, in_pair_out, between_out, own_out):
    def step(second_core, second_chip):
        left_out, right_out = (in_pair_out, between_out) if second_chip else (between_out, in_pair_out)
        if second_core:
            left_out[...] = (far_left[...].astype(jnp.float32) + near[0].astype(jnp.float32)).astype(
                left_out.dtype
            )
            right_out[...] = far_right[...]
            own_out[...] = own[...] + near[1].astype(jnp.float32)
        else:
            left_out[...] = far_left[...]
            right_out[...] = (far_right[...].astype(jnp.float32) + near[1].astype(jnp.float32)).astype(
                right_out.dtype
            )
            own_out[...] = own[...] + near[0].astype(jnp.float32)

    for_each_place(step)


def choose_kernel(in_pair, between, out_ref):
    core, chip = place()

    @pl.when(core == chip)
    def _():
        out_ref[...] = in_pair[...]

    @pl.when(core != chip)
    def _():
        out_ref[...] = between[...]


def backward_kernel(
    src_ref,
    dst_ref,
    count_ref,
    both_ref,
    in_pair,
    between,
    partner,
    passed,
    tiles_ref,
    out_ref,
    gs,
    acc,
):
    tile_blk = acc.shape[0]
    slots = gs.shape[0] - 1
    feat_rows = acc.shape[1]

    def lay(k, ref):
        for r in range(tile_blk):
            gs[k * tile_blk + r] = ref[r // 2, :, (r % 2) * TILE : (r % 2 + 1) * TILE]

    def lay_all(second_core, second_chip):
        lay(0, in_pair if second_chip else between)
        lay(SPAN - 1, partner if second_core else passed)
        lay(SPAN + 1, passed if second_core else partner)
        lay(2 * SPAN, between if second_chip else in_pair)

    lay(SPAN, both_ref.at[:, feat_rows:, :])
    for_each_place(lay_all)
    gs[slots] = jnp.zeros(gs.shape[1:], gs.dtype)
    for r in range(tile_blk):
        acc[r] = both_ref[r // 2, :feat_rows, (r % 2) * TILE : (r % 2 + 1) * TILE].astype(jnp.float32)
    count = count_ref[0]

    def step(i, _):
        parts = []
        for b in range(BATCH):
            s = i * BATCH + b
            d = jnp.where(s < count, dst_ref[0, s], slots)
            parts.append(jnp.dot(gs[d], tiles_ref[s], preferred_element_type=jnp.float32))
        for b in range(BATCH):
            acc[src_ref[0, i * BATCH + b]] += parts[b]
        return 0

    lax.fori_loop(0, batches_of(count), step, 0)
    for r in range(tile_blk):
        out_ref[:, r * TILE : (r + 1) * TILE] = acc[r].astype(out_ref.dtype)


def join_kernel(x_ref, *refs):
    pieces, out_ref = refs[:-1], refs[-1]
    rows = x_ref.shape[0]
    width = out_ref.shape[2]
    for j in range(out_ref.shape[0]):
        out_ref[j, :rows, :] = x_ref[:, j * width : (j + 1) * width]
        total = pieces[0][j].astype(jnp.float32)
        for piece in pieces[1:]:
            total = total + piece[j].astype(jnp.float32)
        out_ref[j, rows:, :] = total.astype(out_ref.dtype)


def dense_kernel(both_ref, ws_ref, wn_ref, og_ref, out_hbm, grads_ref, out_ref, sem):
    groups, twice, width = both_ref.shape
    rows = twice // 2
    x = both_ref[:, :rows, :].reshape(groups * rows, width)
    agg = both_ref[:, rows:, :].reshape(groups * rows, width)
    ws, wn = ws_ref[...], wn_ref[...]
    pre = jnp.dot(ws, x, preferred_element_type=jnp.float32) + jnp.dot(
        wn, agg, preferred_element_type=jnp.float32
    )
    s = jax.nn.sigmoid(pre)
    out_ref[...] = (pre * s).astype(out_ref.dtype)
    out_copy = pltpu.make_async_copy(out_ref, out_hbm, sem)
    out_copy.start()
    grad_pre = (og_ref[...].astype(jnp.float32) * s * (1.0 + pre * (1.0 - s))).astype(jnp.bfloat16)
    turned = (((0,), (0,)), ((), ()))
    grad_self = lax.dot_general(ws, grad_pre, turned, preferred_element_type=jnp.float32)
    grad_agg = lax.dot_general(wn, grad_pre, turned, preferred_element_type=jnp.float32)
    grads_ref[:, :rows, :] = grad_self.astype(jnp.bfloat16).reshape(groups, rows, width)
    grads_ref[:, rows:, :] = grad_agg.astype(jnp.bfloat16).reshape(groups, rows, width)
    out_copy.wait()


def body(features, self_weight, neigh_weight, tiles, tile_src, tile_dst, tile_count, out_grad):
    feat_rows, block_nodes = features.shape
    tile_blk = block_nodes // TILE
    slots = (2 * SPAN + 1) * tile_blk
    slot_count = tiles.shape[1]
    groups = lax.axis_size("feat")
    width = block_nodes // groups
    piece = (groups, feat_rows, width)
    both = (groups, 2 * feat_rows, width)
    local_tiles = tiles[0]
    params = pltpu.CompilerParams(vmem_limit_bytes=24 * 1024 * 1024)
    tile_flops = 2 * slot_count * feat_rows * TILE * TILE
    tile_bytes = slot_count * TILE * TILE * 2

    bf16_piece = jax.ShapeDtypeStruct(piece, jnp.bfloat16)
    f32_piece = jax.ShapeDtypeStruct(piece, jnp.float32)
    far_left, near, own, far_right, held = pl.pallas_call(
        forward_kernel,
        out_shape=[
            bf16_piece,
            jax.ShapeDtypeStruct((2,) + piece, jnp.bfloat16),
            f32_piece,
            bf16_piece,
            jax.ShapeDtypeStruct(local_tiles.shape, jnp.bfloat16),
        ],
        in_specs=[SMEM] + [HBM] * 4,
        out_specs=[VMEM] * 5,
        scratch_shapes=[
            pltpu.SMEM(tile_src.shape, jnp.int32),
            pltpu.SMEM(tile_dst.shape, jnp.int32),
            pltpu.VMEM(features.shape, jnp.bfloat16),
            pltpu.VMEM((tile_blk, feat_rows, TILE), jnp.bfloat16),
            pltpu.VMEM((slots + 1, feat_rows, TILE), jnp.float32),
            pltpu.SemaphoreType.DMA((3,)),
            pltpu.SemaphoreType.DMA((slot_count // BATCH,)),
        ],
        compiler_params=params,
        cost_estimate=pl.CostEstimate(flops=tile_flops, bytes_accessed=tile_bytes, transcendentals=0),
        name="tiles_forward",
    )(tile_count, *(in_hbm(a) for a in (tile_src, tile_dst, features, local_tiles)))

    in_pair, between, own = pl.pallas_call(
        relay_kernel,
        out_shape=[bf16_piece, bf16_piece, f32_piece],
        in_specs=[VMEM] * 4,
        out_specs=[VMEM] * 3,
        compiler_params=params,
        name="relay",
    )(far_left, swapped(near), own, far_right)
    beside = pl.pallas_call(
        join_kernel,
        out_shape=jax.ShapeDtypeStruct(both, jnp.bfloat16),
        in_specs=[VMEM] * 4,
        out_specs=VMEM,
        compiler_params=params,
        name="join",
    )(features, own, chips_swapped(between, 1), chips_swapped(in_pair, 0))
    rows = lax.all_to_all(beside, "feat", split_axis=0, concat_axis=0, tiled=True)
    output, grads = pl.pallas_call(
        dense_kernel,
        out_shape=[
            jax.ShapeDtypeStruct(out_grad.shape, jnp.bfloat16),
            jax.ShapeDtypeStruct(both, jnp.bfloat16),
        ],
        in_specs=[VMEM] * 4,
        out_specs=[HBM, VMEM],
        scratch_shapes=[pltpu.VMEM(out_grad.shape, jnp.bfloat16), pltpu.SemaphoreType.DMA],
        compiler_params=params,
        name="dense",
    )(rows, self_weight, neigh_weight, out_grad)
    cols = lax.all_to_all(grads, "feat", split_axis=0, concat_axis=0, tiled=True)
    agg = cols[:, feat_rows:, :]
    in_pair = chips_swapped(agg, 0)
    between = chips_swapped(agg, 1)
    partner = swapped(agg)
    passed = swapped(
        pl.pallas_call(
            choose_kernel,
            out_shape=bf16_piece,
            in_specs=[VMEM] * 2,
            out_specs=VMEM,
            compiler_params=params,
            name="choose",
        )(in_pair, between)
    )
    grad_features = pl.pallas_call(
        backward_kernel,
        out_shape=jax.ShapeDtypeStruct(features.shape, jnp.bfloat16),
        in_specs=[SMEM] * 3 + [VMEM] * 6,
        out_specs=VMEM,
        scratch_shapes=[
            pltpu.VMEM((slots + 1, feat_rows, TILE), jnp.bfloat16),
            pltpu.VMEM((tile_blk, feat_rows, TILE), jnp.float32),
        ],
        compiler_params=params,
        cost_estimate=pl.CostEstimate(flops=tile_flops, bytes_accessed=tile_bytes, transcendentals=0),
        name="tiles_backward",
    )(
        tile_src, tile_dst, tile_count, cols, in_pair, between, partner, passed, held
    )
    return (output, grad_features)


def solution(mesh):
    return jax.shard_map(
        body,
        mesh=mesh,
        in_specs=(
            P("feat", "node"),
            P(),
            P(),
            P("node", None, None, None),
            P("node", None),
            P("node", None),
            P("node"),
            P(None, ("node", "feat")),
        ),
        out_specs=(P(None, ("node", "feat")), P("feat", "node")),
        check_vma=False,
    )
```
